128 devices in a mesh: row: 8 (over y, core), col: 16 (over z, x).
Axes of the slice: x: 4, y: 4, z: 4, core: 2. Of those that a mesh axis runs over, the one named last changes fastest.
Arguments:
- child_fronts: float32 [20, 512, 20, 1024], P(None, 'col', None, 'row'), as said below
- parent_diagonal: float32 [16384], replicated, may hold values from 0.5 to 4
- block_maps: int32 [2, 20], replicated, may hold values from 0 to 31, as said below
Outputs:
- factored: float32 [16384, 16384], P('row', 'col')
The draws below stay inside these ranges and needn't reach their ends.
Inputs may be any that keep to these rules, and one draw needn't show every extreme that they name: `child_fronts`: each child's matrix is symmetric and positive definite. `block_maps`: each row names 20 distinct front blocks in increasing order; every one of the 32 front blocks is named by at least one row, and exactly 8 of them by both rows.
All inputs are finite; a program needn't handle non-finite values.
Results may differ from the reference program's by a relative error of at most 0.0001.
Values sent between devices are 32-bit elements; how exact they have to be, the bound alone decides.
No kernel may reach another device: no remote copies, remote signals or barrier semaphores. Data moves between devices by JAX's collectives and lax.ppermute only.
A program may use at most 128 MiB of HBM per device.

```python
import math
import jax
import jax.numpy as jnp
from jax import lax

B = 512
F = 16384
NC = 10240
NB = 32
NCB = 20
N_ROW = 8
N_COL = 16


length_scale = 0.15


nugget_level = 1.0


def draw_child_fronts(key, part):
    matrices = []
    for which_child in range(2):
        subkey = jax.random.fold_in(key, 11 + which_child)
        point_key, scale_key = jax.random.split(subkey)
        points = jax.random.uniform(point_key, (NC, 3), jnp.float32)
        scales = jnp.exp(jax.random.uniform(scale_key, (NC,), jnp.float32, jnp.log(0.5), jnp.log(5.0)))
        squared = jnp.zeros((NC, NC), jnp.float32)
        for coord in range(3):
            spread = points[:, None, coord] - points[None, :, coord]
            squared = squared + spread * spread
        kernel = jnp.exp(-jnp.sqrt(squared) / length_scale)
        positions = jnp.arange(NC, dtype=jnp.int32)
        kernel = kernel + jnp.where(positions[:, None] == positions[None, :], nugget_level, 0.0)
        roots = jnp.sqrt(scales)
        matrix = roots[:, None] * kernel * roots[None, :]
        matrices.append(matrix.reshape(NCB, B, NCB, B))
    return jnp.concatenate(matrices, axis=3).astype(jnp.float32)


def draw_block_maps(key, part):
    shuffled = jax.random.permutation(jax.random.fold_in(key, 5), NB).astype(jnp.int32)
    first_map = jnp.sort(shuffled[:NCB])
    second_map = jnp.sort(shuffled[NB - NCB:])
    return jnp.stack([first_map, second_map], axis=0).astype(jnp.int32)


def setup_inputs(seed: int = 0) -> dict:
    seeds = jax.random.split(jax.random.key(seed), 4)
    child_fronts = draw_child_fronts(jax.random.fold_in(seeds[3], 71), 0)
    parent_diagonal = jnp.clip(jnp.exp(jax.random.uniform(seeds[1], (F,), jnp.float32, math.log(0.5), math.log(4.0))), 0.5, 4.0)
    block_maps = draw_block_maps(jax.random.fold_in(seeds[3], 71), 0)
    return dict(child_fronts=child_fronts, parent_diagonal=parent_diagonal, block_maps=block_maps)


def reference(child_fronts, parent_diagonal, block_maps):
    order_full = NB * B
    assembled = jnp.zeros((NB, NB, B, B), jnp.float32)
    for which_child in range(2):
        child_block = child_fronts[:, :, :, which_child * B:(which_child + 1) * B]
        child_block = jnp.transpose(child_block, (0, 2, 1, 3))
        placing = block_maps[which_child].astype(jnp.int32)
        assembled = assembled.at[placing[:, None], placing[None, :]].add(child_block)
    frontal = jnp.transpose(assembled, (0, 2, 1, 3)).reshape(order_full, order_full)
    indices = jnp.arange(order_full, dtype=jnp.int32)
    frontal = frontal.at[indices, indices].add(parent_diagonal)
    for panel_index in range(2):
        start_row = panel_index * B
        stop_row = start_row + B
        factor_block = jnp.linalg.cholesky(frontal[start_row:stop_row, start_row:stop_row])
        below_rows = frontal[stop_row:, start_row:stop_row]
        solved = jax.scipy.linalg.solve_triangular(factor_block, below_rows.T, lower=True).T
        trailing = frontal[stop_row:, stop_row:] - jnp.dot(solved.astype(jnp.float32), solved.T.astype(jnp.float32), precision=lax.Precision.HIGHEST, preferred_element_type=jnp.float32)
        frontal = frontal.at[stop_row:, stop_row:].set(trailing)
        frontal = frontal.at[start_row:stop_row, start_row:stop_row].set(factor_block)
        frontal = frontal.at[stop_row:, start_row:stop_row].set(solved)
        frontal = frontal.at[:start_row, start_row:stop_row].set(0.0)
        frontal = frontal.at[start_row:stop_row, stop_row:].set(0.0)
    shaped = frontal.reshape(NB // N_ROW, N_ROW, B, NB // N_COL, N_COL, B)
    shaped = jnp.transpose(shaped, (1, 0, 2, 4, 3, 5))
    return shaped.reshape(order_full, order_full)
```

```python
import functools

import jax
import jax.numpy as jnp
from jax import lax
from jax.experimental import pallas as pl
from jax.experimental.pallas import tpu as pltpu
from jax.sharding import PartitionSpec as P

B = 512
NB = 32
NCB = 20
N_ROW = 8
N_COL = 16
W = 2 * B
H = 16
SL = 128
CB = 128
ST = 16
HI = lax.Precision.HIGHEST
F32 = jnp.float32
VMEM = pltpu.VMEM
MIB = 1024 * 1024


def whole():
    return pl.BlockSpec(memory_space=VMEM)


def smem():
    return pl.BlockSpec(memory_space=pltpu.SMEM)


def params(mib):
    return pltpu.CompilerParams(vmem_limit_bytes=mib * MIB)


def cost(flops, nbytes):
    return pl.CostEstimate(flops=int(flops), bytes_accessed=int(nbytes), transcendentals=0)


def invert_maps(maps_ref, inv_ref):
    def clear(i, _):
        inv_ref[0, i] = -1
        inv_ref[1, i] = -1
        return 0

    lax.fori_loop(0, NB, clear, 0)

    def fill(b, _):
        inv_ref[0, maps_ref[0, b]] = b
        inv_ref[1, maps_ref[1, b]] = b
        return 0

    lax.fori_loop(0, NCB, fill, 0)


def split_kernel(child_ref, keep_ref, send_ref):
    half = lax.axis_index("row") // (N_ROW // 2)
    turned = jnp.swapaxes(child_ref[0], 0, 1)
    first = turned[:, :H]
    second = turned[:, H:]
    keep_ref[0] = jnp.where(half == 0, first, second)
    send_ref[0] = jnp.where(half == 0, second, first)


def split_child(child):
    shape = jax.ShapeDtypeStruct((NCB, NCB, H, SL), F32)
    spec = pl.BlockSpec((1, NCB, H, SL), lambda a: (a, 0, 0, 0))
    return pl.pallas_call(
        split_kernel,
        grid=(NCB,),
        in_specs=[pl.BlockSpec((1, 2 * H, NCB, SL), lambda a: (a, 0, 0, 0))],
        out_specs=[spec, spec],
        out_shape=[shape, shape],
        compiler_params=params(32),
        cost_estimate=cost(0, 14 * MIB),
        name="split_child",
    )(child)


def panel_kernel(maps_ref, keep_ref, send_ref, xy_ref, d_ref, inv_ref):
    child = lax.axis_index("row") // (N_ROW // 2)
    invert_maps(maps_ref, inv_ref)

    def tile(front_row, front_col, half):
        a = inv_ref[child, front_row]
        b = inv_ref[child, front_col]
        ok = jnp.logical_and(a >= 0, b >= 0)
        a = jnp.maximum(a, 0)
        b = jnp.maximum(b, 0)
        value = jnp.where(half == child, keep_ref[a, b], send_ref[a, b])
        return jnp.where(ok, value, 0.0)

    def across(col, _):
        part, blk, half = col // 4, (col // 2) % 2, col % 2
        for row in range(N_ROW):
            xy_ref[row, col, 0] = tile(row + N_ROW * part, blk, half)
            xy_ref[row, col, 1] = tile(row // 4, col + N_COL * ((row // 2) % 2), row % 2)
        return 0

    lax.fori_loop(0, N_COL, across, 0)
    for blk in range(2):
        for other in range(2):
            for half in range(2):
                d_ref[blk, other, half] = tile(blk, other, half)


def panel_pieces(maps, keep, send):
    return pl.pallas_call(
        panel_kernel,
        in_specs=[smem(), whole(), whole()],
        out_specs=[whole(), whole()],
        out_shape=[
            jax.ShapeDtypeStruct((N_ROW, N_COL, 2, H, SL), F32),
            jax.ShapeDtypeStruct((2, 2, 2, H, SL), F32),
        ],
        scratch_shapes=[pltpu.SMEM((2, NB), jnp.int32)],
        compiler_params=params(32),
        cost_estimate=cost(0, 9 * MIB),
        name="panel_pieces",
    )(maps, keep, send)


def pack_kernel(maps_ref, own_ref, other_ref, out_ref, inv_ref):
    child = lax.axis_index("row") // (N_ROW // 2)
    row = pl.program_id(0)

    @pl.when(row == 0)
    def _():
        invert_maps(maps_ref, inv_ref)

    def value(ref, c, i, j):
        a = inv_ref[c, i]
        b = inv_ref[c, j]
        ok = jnp.logical_and(a >= 0, b >= 0)
        return jnp.where(ok, ref[jnp.maximum(a, 0), jnp.maximum(b, 0)], 0.0)

    def across(col, _):
        for part in range(4):
            for side in range(2):
                i = row + N_ROW * part
                j = col + N_COL * side
                out_ref[0, col, part, side] = value(own_ref, child, i, j) + value(
                    other_ref, 1 - child, i, j
                )
        return 0

    lax.fori_loop(0, N_COL, across, 0)


def pack(maps, own, other):
    return pl.pallas_call(
        pack_kernel,
        grid=(N_ROW,),
        in_specs=[smem(), whole(), whole()],
        out_specs=pl.BlockSpec((1, N_COL, 4, 2, H, SL), lambda r: (r, 0, 0, 0, 0, 0)),
        out_shape=jax.ShapeDtypeStruct((N_ROW, N_COL, 4, 2, H, SL), F32),
        scratch_shapes=[pltpu.SMEM((2, NB), jnp.int32)],
        compiler_params=params(32),
        cost_estimate=cost(0, 16 * MIB),
        name="pack",
    )(maps, own, other)


def dot_tn(a, b):
    return lax.dot_general(a, b, (((0,), (0,)), ((), ())), precision=HI, preferred_element_type=F32)


def dot_nn(a, b):
    return lax.dot_general(a, b, (((1,), (0,)), ((), ())), precision=HI, preferred_element_type=F32)


def dot_nt(a, b):
    return lax.dot_general(a, b, (((1,), (1,)), ((), ())), precision=HI, preferred_element_type=F32)


def factor_block(t_ref, w_ref, s_ref, e_ref):
    for p in range(CB // ST):
        lo = p * ST
        rows = lax.broadcasted_iota(jnp.int32, (ST, CB), 0)
        cols = lax.broadcasted_iota(jnp.int32, (ST, CB), 1)
        ident = jnp.where(cols == rows + lo, 1.0, 0.0).astype(F32)
        s = jnp.concatenate([t_ref[lo : lo + ST, :], ident], axis=1)
        if p:
            s = s - dot_tn(w_ref[0:lo, lo : lo + ST], w_ref[0:lo, :])
        s_ref[...] = s
        for c in range(ST):
            e_ref[c] = jnp.broadcast_to(s[:, lo + c : lo + c + 1], (ST, CB))
        e = {}
        for c in range(ST):
            for r in range(c, ST):
                e[r, c] = e_ref[c, r : r + 1, :]
        done = []
        for j in range(ST):
            inv = lax.rsqrt(e[j, j])
            for r in range(j + 1, ST):
                e[r, j] = e[r, j] * inv
            for c in range(j + 1, ST):
                for r in range(c, ST):
                    e[r, c] = e[r, c] - e[r, j] * e[c, j]
            u = s_ref[j : j + 1, :]
            for m in range(j):
                u = u - jnp.concatenate([e[j, m], e[j, m]], axis=1) * done[m]
            u = u * jnp.concatenate([inv, inv], axis=1)
            done.append(u)
            w_ref[lo + j : lo + j + 1, :] = u


def chol_kernel(d_ref, diag_ref, l_ref, linv_ref, a_s, w_s, s_s, e_s, t_s):
    n = W
    nb = n // CB
    a_s[...] = jnp.zeros_like(a_s)
    for src in range(N_COL):
        for blk in range(2):
            lo = blk * B + src * 2 * H
            a_s[lo : lo + 2 * H, :] = d_ref[src, blk]
    low = lax.broadcasted_iota(jnp.int32, (CB, CB), 0)
    high = lax.broadcasted_iota(jnp.int32, (CB, CB), 1)
    l_ref[...] = jnp.zeros_like(l_ref)
    linv_ref[...] = jnp.zeros_like(linv_ref)

    def block(i):
        return pl.ds(pl.multiple_of(i * CB, CB), CB)

    def add_diagonal(k, _):
        ks = block(k)
        a_s[ks, ks] = a_s[ks, ks] + jnp.where(low == high, diag_ref[0:1, ks], 0.0)
        return 0

    lax.fori_loop(0, nb, add_diagonal, 0)

    def step(k, _):
        ks = block(k)
        t_s[...] = a_s[ks, ks]
        factor_block(t_s, w_s, s_s, e_s)
        upper = jnp.where(low <= high, w_s[:, 0:CB], 0.0)
        lower_inverse = jnp.where(low >= high, w_s[:, CB:], 0.0)

        def solve(j, _):
            js = block(j)
            r = dot_nn(lower_inverse, a_s[ks, js])
            a_s[ks, js] = r
            l_ref[js, ks] = r.T
            return 0

        lax.fori_loop(k + 1, nb, solve, 0)
        l_ref[ks, ks] = upper.T

        def update(i, _):
            ins = block(i)
            f = a_s[ks, ins]

            def inner(j, _):
                js = block(j)
                a_s[ins, js] = a_s[ins, js] - dot_tn(f, a_s[ks, js])
                return 0

            lax.fori_loop(i, nb, inner, 0)
            return 0

        lax.fori_loop(k + 1, nb, update, 0)
        linv_ref[ks, ks] = lower_inverse
        return 0

    lax.fori_loop(0, nb, step, 0)
    for i in range(1, nb):
        lo = i * CB
        acc = dot_nn(l_ref[lo : lo + CB, 0:lo], linv_ref[0:lo, 0:lo])
        linv_ref[lo : lo + CB, 0:lo] = -dot_nn(linv_ref[lo : lo + CB, lo : lo + CB], acc)


def cholesky(d, diag):
    return pl.pallas_call(
        chol_kernel,
        in_specs=[whole(), whole()],
        out_specs=[whole(), whole()],
        out_shape=[jax.ShapeDtypeStruct((W, W), F32)] * 2,
        scratch_shapes=[
            VMEM((W, W), F32),
            VMEM((CB, 2 * CB), F32),
            VMEM((ST, 2 * CB), F32),
            VMEM((ST, ST, CB), F32),
            VMEM((CB, CB), F32),
        ],
        compiler_params=params(40),
        cost_estimate=cost(5e10, 12 * MIB),
        name="leading_cholesky",
    )(d, diag)


def across_kernel(y_ref, linv_ref, high_ref, low_ref, a_s):
    for blk in range(2):
        for half in range(2):
            for src in range(N_COL):
                lo = blk * B + src * 2 * H + half * H
                a_s[lo : lo + H, :] = y_ref[blk, 0, half, src]
    step = 256
    for t in range(W // step):
        lo, hi = t * step, (t + 1) * step
        r = dot_nn(linv_ref[lo:hi, 0:hi], a_s[0:hi, :])
        high = r.astype(jnp.bfloat16)
        high_ref[lo:hi, :] = high
        low_ref[lo:hi, :] = (r - high.astype(F32)).astype(jnp.bfloat16)


def solve_across(y, linv):
    out = jax.ShapeDtypeStruct((W, 2 * B), jnp.bfloat16)
    spec = pl.BlockSpec((W, B), lambda q: (0, q))
    return pl.pallas_call(
        across_kernel,
        grid=(2,),
        in_specs=[
            pl.BlockSpec((2, 1, 2, N_COL, H, B), lambda q: (0, q, 0, 0, 0, 0)),
            whole(),
        ],
        out_specs=[spec, spec],
        out_shape=[out, out],
        scratch_shapes=[VMEM((W, B), F32)],
        compiler_params=params(40),
        cost_estimate=cost(8e9, 12 * MIB),
        name="solve_across",
    )(y, linv)


def product_kernel(x_ref, linv_ref, l_ref, high_ref, low_ref, p_ref, a_s, f_s):
    row = lax.axis_index("row")
    col = lax.axis_index("col")
    part = pl.program_id(0)
    front_row = row + N_ROW * part

    @pl.when(front_row >= 2)
    def _():
        for blk in range(2):
            for half in range(2):
                for src in range(N_COL):
                    lo = src * 2 * H + half * H
                    a_s[lo : lo + H, blk * B : (blk + 1) * B] = x_ref[0, blk, half, src]
        step = 256
        for t in range(W // step):
            lo, hi = t * step, (t + 1) * step
            f_s[:, lo:hi] = dot_nt(a_s[:, 0:hi], linv_ref[lo:hi, 0:hi])
        f = f_s[...]
        f_high = f.astype(jnp.bfloat16)
        f_low = (f - f_high.astype(F32)).astype(jnp.bfloat16)

        def mul(x, y):
            return lax.dot_general(x, y, (((1,), (0,)), ((), ())), preferred_element_type=F32)

        for t in range(W // step):
            ts = slice(t * step, (t + 1) * step)
            high = high_ref[:, ts]
            p_ref[:, ts] = mul(f_high, high) + (mul(f_low, high) + mul(f_high, low_ref[:, ts]))

    @pl.when(front_row < 2)
    def _():
        p_ref[...] = jnp.zeros_like(p_ref)
        f_s[...] = l_ref[pl.ds(pl.multiple_of(jnp.minimum(front_row, 1) * B, B), B), :]

    @pl.when(col == 0)
    def _():
        p_ref[:, 0:B] = -f_s[:, 0:B]

    @pl.when(col == 1)
    def _():
        p_ref[:, 0:B] = -f_s[:, B:]


def panel_product(x, linv, lower, high, low):
    return pl.pallas_call(
        product_kernel,
        grid=(4,),
        in_specs=[
            pl.BlockSpec((1, 2, 2, N_COL, H, B), lambda s: (s, 0, 0, 0, 0, 0)),
            whole(),
            whole(),
            whole(),
            whole(),
        ],
        out_specs=pl.BlockSpec((B, 2 * B), lambda s: (s, 0)),
        out_shape=jax.ShapeDtypeStruct((4 * B, 2 * B), F32),
        scratch_shapes=[VMEM((B, W), F32), VMEM((B, W), F32)],
        compiler_params=params(50),
        cost_estimate=cost(2.5e10, 30 * MIB),
        name="panel_product",
    )(x, linv, lower, high, low)


def finish_kernel(recv_ref, p_ref, diag_ref, out_ref):
    row = lax.axis_index("row")
    col = lax.axis_index("col")
    front_row = row + N_ROW * pl.program_id(0)
    front_col = col + N_COL * pl.program_id(1)
    inside = jnp.logical_and(front_row >= 2, front_col >= 2)
    for half in range(2):
        for js in range(4):
            cs = slice(js * SL, (js + 1) * SL)
            for src in range(N_COL):
                lo = src * 2 * H + half * H
                value = recv_ref[half * 4 + js, src, 0, 0]
                out_ref[lo : lo + H, cs] = jnp.where(inside, value, 0.0) - p_ref[lo : lo + H, cs]

    @pl.when(jnp.logical_and(inside, front_row == front_col))
    def _():
        for t in range(B // SL):
            ts = slice(t * SL, (t + 1) * SL)
            eye = lax.broadcasted_iota(jnp.int32, (SL, SL), 0) == lax.broadcasted_iota(
                jnp.int32, (SL, SL), 1
            )
            d = diag_ref[front_row, :, ts]
            out_ref[ts, ts] = out_ref[ts, ts] + jnp.where(eye, d, 0.0)


def finish(received, product, diag):
    spec = pl.BlockSpec((B, B), lambda s, q: (s, q))
    return pl.pallas_call(
        finish_kernel,
        grid=(4, 2),
        in_specs=[
            pl.BlockSpec((N_ROW, N_COL, 1, 1, H, SL), lambda s, q: (0, 0, s, q, 0, 0)),
            spec,
            whole(),
        ],
        out_specs=spec,
        out_shape=jax.ShapeDtypeStruct((4 * B, 2 * B), F32),
        compiler_params=params(32),
        cost_estimate=cost(0, 24 * MIB),
        name="finish",
    )(received, product, diag)


def shards(child_fronts, parent_diagonal, block_maps):
    half_rows = N_ROW // 2
    keep, send = split_child(child_fronts)
    other = lax.ppermute(send, "row", [(i, (i + half_rows) % N_ROW) for i in range(N_ROW)])
    xy, d = panel_pieces(block_maps, keep, send)

    d = lax.all_gather(d, "row", axis=0, tiled=False)
    d = d[:half_rows] + d[half_rows:]
    d = d.transpose(1, 3, 4, 2, 0, 5).reshape(2, 2 * H, W)
    d = lax.all_gather(d, "col", axis=0, tiled=False)
    lower, inverse = cholesky(d, parent_diagonal[: 2 * B].reshape(1, 2 * B))

    xy = lax.all_to_all(
        xy.reshape(N_ROW * N_COL, 2, H, SL), ("row", "col"), split_axis=0, concat_axis=0, tiled=True
    )
    xy = xy.reshape(2, half_rows, N_COL, 2, H, SL)
    xy = (xy[0] + xy[1]).transpose(2, 1, 3, 0, 4).reshape(2, N_COL, H, B)
    y = lax.all_gather(xy[1], "row", axis=0, tiled=False).reshape(2, 2, 2, N_COL, H, B)
    x = lax.all_gather(xy[0], "col", axis=0, tiled=False).reshape(4, 2, 2, N_COL, H, B)

    packed = pack(block_maps, keep, other)
    received = lax.all_to_all(
        packed.reshape(N_ROW * N_COL, 4, 2, H, SL),
        ("row", "col"),
        split_axis=0,
        concat_axis=0,
        tiled=True,
    ).reshape(N_ROW, N_COL, 4, 2, H, SL)

    high, low = solve_across(y, inverse)
    product = panel_product(x, inverse, lower, high, low)
    return finish(received, product, parent_diagonal.reshape(NB, 1, B))


def solution(mesh):
    return jax.shard_map(
        shards,
        mesh=mesh,
        in_specs=(P(None, "col", None, "row"), P(), P()),
        out_specs=P("row", "col"),
        check_vma=False,
    )
```

```python
import functools

import jax
import jax.numpy as jnp
from jax import lax
from jax.experimental import pallas as pl
from jax.experimental.pallas import tpu as pltpu
from jax.sharding import PartitionSpec as P

B = 512
NB = 32
NCB = 20
N_ROW = 8
N_COL = 16
W = 2 * B
H = 16
SL = 128
CB = 128
ST = 16
HI = lax.Precision.HIGHEST
F32 = jnp.float32
VMEM = pltpu.VMEM
MIB = 1024 * 1024


def whole():
    return pl.BlockSpec(memory_space=VMEM)


def smem():
    return pl.BlockSpec(memory_space=pltpu.SMEM)


def params(mib):
    return pltpu.CompilerParams(vmem_limit_bytes=mib * MIB)


def cost(flops, nbytes):
    return pl.CostEstimate(flops=int(flops), bytes_accessed=int(nbytes), transcendentals=0)


def invert_maps(maps_ref, inv_ref):
    def clear(i, _):
        inv_ref[0, i] = NCB
        inv_ref[1, i] = NCB
        return 0

    lax.fori_loop(0, NB, clear, 0)

    def fill(b, _):
        inv_ref[0, maps_ref[0, b]] = b
        inv_ref[1, maps_ref[1, b]] = b
        return 0

    lax.fori_loop(0, NCB, fill, 0)


TRI = (NCB - 1) * (NCB - 2) // 2


def split_panel_kernel(child_ref, keep_ref, send_ref):
    half = lax.axis_index("row") // (N_ROW // 2)
    keep = pl.ds(pl.multiple_of(half * H, H), H)
    send = pl.ds(pl.multiple_of((1 - half) * H, H), H)
    for b in range(2):
        keep_ref[b] = child_ref[:, b, keep]
        send_ref[b] = child_ref[:, b, send]


def split_panel(child):
    shape = jax.ShapeDtypeStruct((2, NCB, H, SL), F32)
    return pl.pallas_call(
        split_panel_kernel,
        grid=(1,),
        in_specs=[pl.BlockSpec((NCB, 2, 2 * H, SL), lambda g: (0, 0, 0, 0))],
        out_specs=[whole(), whole()],
        out_shape=[shape, shape],
        compiler_params=params(58),
        cost_estimate=cost(0, 2 * MIB),
        name="split_panel",
    )(child)


def split_rest_kernel(child_ref, keep_ref, send_ref):
    half = lax.axis_index("row") // (N_ROW // 2)
    keep = pl.ds(pl.multiple_of(half * H, H), H)
    send = pl.ds(pl.multiple_of((1 - half) * H, H), H)
    for a in range(2, NCB):
        at = (a - 1) * (a - 2) // 2
        keep_ref[at : at + a - 1] = child_ref[a, 2 : a + 1, keep]
        send_ref[at : at + a - 1] = child_ref[a, 2 : a + 1, send]


def split_rest(child):
    shape = jax.ShapeDtypeStruct((TRI, H, SL), F32)
    return pl.pallas_call(
        split_rest_kernel,
        in_specs=[whole()],
        out_specs=[whole(), whole()],
        out_shape=[shape, shape],
        compiler_params=params(58),
        cost_estimate=cost(0, 10 * MIB),
        name="split_rest",
    )(child)


def panel_kernel(maps_ref, keep_ref, other_ref, xd_ref, y_ref, sum_ref, inv_ref):
    child = lax.axis_index("row") // (N_ROW // 2)
    invert_maps(maps_ref, inv_ref)

    def tile(ref, c, i, blk):
        a = inv_ref[c, i]
        b = inv_ref[c, blk]
        ok = jnp.maximum(a, b) < NCB
        return jnp.where(ok, ref[jnp.minimum(b, 1), jnp.minimum(a, NCB - 1)], 0.0)

    def collect(i, _):
        for blk in range(2):
            sum_ref[blk, i] = tile(keep_ref, child, i, blk) + tile(other_ref, 1 - child, i, blk)
        return 0

    lax.fori_loop(0, NB, collect, 0)
    for row in range(N_ROW):
        for part in range(4):
            for blk in range(2):
                xd_ref[row, part * 2 + blk] = sum_ref[blk, row + N_ROW * part]
        for at, (blk, other) in enumerate(((0, 0), (0, 1), (1, 1))):
            xd_ref[row, 8 + at] = sum_ref[other, blk]
    for col in range(N_COL):
        for side in range(2):
            for blk in range(2):
                y_ref[col, side, blk] = sum_ref[blk, col + N_COL * side]


def panel_pieces(maps, keep, other):
    return pl.pallas_call(
        panel_kernel,
        in_specs=[smem(), whole(), whole()],
        out_specs=[whole(), whole()],
        out_shape=[
            jax.ShapeDtypeStruct((N_ROW, 11, H, SL), F32),
            jax.ShapeDtypeStruct((N_COL, 2, 2, H, SL), F32),
        ],
        scratch_shapes=[VMEM((2, NB, H, SL), F32), pltpu.SMEM((2, NB), jnp.int32)],
        compiler_params=params(58),
        cost_estimate=cost(0, 3 * MIB),
        name="panel_pieces",
    )(maps, keep, other)


WIDE = NCB + 1


def pack_kernel(maps_ref, p0_ref, p1_ref, r0_ref, r1_ref, out_ref, t0_ref, t1_ref, inv_ref):
    child = lax.axis_index("row") // (N_ROW // 2)
    row = pl.program_id(0)

    @pl.when(row == 0)
    def _():
        invert_maps(maps_ref, inv_ref)
        for p_ref, r_ref, t_ref in ((p0_ref, r0_ref, t0_ref), (p1_ref, r1_ref, t1_ref)):
            for a in range(NCB):
                for b in range(min(a + 1, 2)):
                    t_ref[a * WIDE + b] = p_ref[b, a]
                if a >= 2:
                    at = (a - 1) * (a - 2) // 2
                    t_ref[a * WIDE + 2 : a * WIDE + a + 1] = r_ref[at : at + a - 1]
            t_ref[NCB * WIDE : WIDE * WIDE] = jnp.zeros((WIDE, H, SL), F32)

    rows = [
        (inv_ref[child, row + N_ROW * part], inv_ref[1 - child, row + N_ROW * part])
        for part in range(4)
    ]

    def across(col, _):
        for side in range(2):
            j0 = inv_ref[child, col + N_COL * side]
            j1 = inv_ref[1 - child, col + N_COL * side]
            for part in range(4):
                i0, i1 = rows[part]
                out_ref[0, col, part, side] = (
                    t0_ref[jnp.maximum(i0, j0) * WIDE + jnp.minimum(i0, j0)]
                    + t1_ref[jnp.maximum(i1, j1) * WIDE + jnp.minimum(i1, j1)]
                )
        return 0

    lax.fori_loop(0, N_COL, across, 0, unroll=2)


def pack(maps, p0, p1, r0, r1):
    return pl.pallas_call(
        pack_kernel,
        grid=(N_ROW,),
        in_specs=[smem(), whole(), whole(), whole(), whole()],
        out_specs=pl.BlockSpec((1, N_COL, 4, 2, H, SL), lambda r: (r, 0, 0, 0, 0, 0)),
        out_shape=jax.ShapeDtypeStruct((N_ROW, N_COL, 4, 2, H, SL), F32),
        scratch_shapes=[
            VMEM((WIDE * WIDE, H, SL), F32),
            VMEM((WIDE * WIDE, H, SL), F32),
            pltpu.SMEM((2, NB), jnp.int32),
        ],
        compiler_params=params(58),
        cost_estimate=cost(0, 16 * MIB),
        name="pack",
    )(maps, p0, p1, r0, r1)


def dot_tn(a, b):
    return lax.dot_general(a, b, (((0,), (0,)), ((), ())), precision=HI, preferred_element_type=F32)


def dot_nn(a, b):
    return lax.dot_general(a, b, (((1,), (0,)), ((), ())), precision=HI, preferred_element_type=F32)


def dot_nt(a, b):
    return lax.dot_general(a, b, (((1,), (1,)), ((), ())), precision=HI, preferred_element_type=F32)


def factor_block(t_ref, w_ref, s_ref, e_ref):
    for p in range(CB // ST):
        lo = p * ST
        rows = lax.broadcasted_iota(jnp.int32, (ST, CB), 0)
        cols = lax.broadcasted_iota(jnp.int32, (ST, CB), 1)
        ident = jnp.where(cols == rows + lo, 1.0, 0.0).astype(F32)
        s = jnp.concatenate([t_ref[lo : lo + ST, :], ident], axis=1)
        if p:
            s = s - dot_tn(w_ref[0:lo, lo : lo + ST], w_ref[0:lo, :])
        s_ref[...] = s
        for c in range(ST):
            e_ref[c] = jnp.broadcast_to(s[:, lo + c : lo + c + 1], (ST, CB))
        e = {}
        for c in range(ST):
            for r in range(c, ST):
                e[r, c] = e_ref[c, r : r + 1, :]
        done = []
        for j in range(ST):
            inv = lax.rsqrt(e[j, j])
            for r in range(j + 1, ST):
                e[r, j] = e[r, j] * inv
            for c in range(j + 1, ST):
                for r in range(c, ST):
                    e[r, c] = e[r, c] - e[r, j] * e[c, j]
            u = s_ref[j : j + 1, :]
            for m in range(j):
                u = u - jnp.concatenate([e[j, m], e[j, m]], axis=1) * done[m]
            u = u * jnp.concatenate([inv, inv], axis=1)
            done.append(u)
            w_ref[lo + j : lo + j + 1, :] = u


def gather_rows(a_s, row, col, piece):
    for src in range(N_COL):
        for dev in range(N_ROW):
            lo = row + src * 2 * H + (dev // 4) * H
            at = col + (dev % 4) * SL
            a_s[lo : lo + H, at : at + SL] = piece(src, dev)


DB = 2 * CB


def chol_kernel(d_ref, diag_ref, l_ref, linv_ref, a_s, w_s, s_s, e_s, t_s):
    nb = W // DB
    for at, (blk, other) in enumerate(((0, 0), (0, 1), (1, 1))):
        gather_rows(a_s, blk * B, other * B, lambda src, dev: d_ref[src, dev, at])
    low = lax.broadcasted_iota(jnp.int32, (CB, CB), 0)
    high = lax.broadcasted_iota(jnp.int32, (CB, CB), 1)
    l_ref[...] = jnp.zeros_like(l_ref)
    linv_ref[...] = jnp.zeros_like(linv_ref)
    for t in range(W // CB):
        ts = slice(t * CB, (t + 1) * CB)
        a_s[ts, ts] = a_s[ts, ts] + jnp.where(low == high, diag_ref[0:1, ts], 0.0)

    def block(i):
        return pl.ds(pl.multiple_of(i * DB, DB), DB)

    def factor():
        factor_block(t_s, w_s, s_s, e_s)
        return jnp.where(low <= high, w_s[:, :CB], 0.0), jnp.where(low >= high, w_s[:, CB:], 0.0)

    def step(k, _):
        ks = block(k)
        k0 = pl.ds(pl.multiple_of(k * DB, CB), CB)
        k1 = pl.ds(pl.multiple_of(k * DB + CB, CB), CB)
        t_s[...] = a_s[k0, k0]
        upper, inverse = factor()
        l_ref[k0, k0] = upper.T
        linv_ref[k0, k0] = inverse
        right = dot_nn(inverse, a_s[k0, k1])
        l_ref[k1, k0] = right.T
        t_s[...] = a_s[k1, k1] - dot_tn(right, right)
        between = dot_tn(right, inverse)
        upper, inverse = factor()
        l_ref[k1, k1] = upper.T
        linv_ref[k1, k1] = inverse
        linv_ref[k1, k0] = -dot_nn(inverse, between)

        def solve(j, _):
            js = block(j)
            r = dot_nn(linv_ref[ks, ks], a_s[ks, js])
            a_s[ks, js] = r
            l_ref[js, ks] = r.T
            return 0

        lax.fori_loop(k + 1, nb, solve, 0)

        def update(i, _):
            ins = block(i)

            def inner(j, _):
                js = block(j)
                a_s[ins, js] = a_s[ins, js] - dot_tn(a_s[ks, ins], a_s[ks, js])
                return 0

            lax.fori_loop(i, nb, inner, 0)
            return 0

        lax.fori_loop(k + 1, nb, update, 0)
        return 0

    lax.fori_loop(0, nb, step, 0)
    for i in range(1, nb):
        lo = i * DB
        acc = dot_nn(l_ref[lo : lo + DB, 0:lo], linv_ref[0:lo, 0:lo])
        linv_ref[lo : lo + DB, 0:lo] = -dot_nn(linv_ref[lo : lo + DB, lo : lo + DB], acc)


def cholesky(d, diag):
    return pl.pallas_call(
        chol_kernel,
        in_specs=[whole(), whole()],
        out_specs=[whole(), whole()],
        out_shape=[jax.ShapeDtypeStruct((W, W), F32)] * 2,
        scratch_shapes=[
            VMEM((W, W), F32),
            VMEM((CB, 2 * CB), F32),
            VMEM((ST, 2 * CB), F32),
            VMEM((ST, ST, CB), F32),
            VMEM((CB, CB), F32),
        ],
        compiler_params=params(58),
        cost_estimate=cost(5e10, 12 * MIB),
        name="leading_cholesky",
    )(d, diag)


def across_kernel(y_ref, linv_ref, high_ref, low_ref, a_s, f_s):
    for blk in range(2):
        gather_rows(a_s, 0, blk * B, lambda src, dev: y_ref[dev, src, 0, blk])
    step = 256
    for t in range(W // step):
        lo, hi = t * step, (t + 1) * step
        f_s[lo:hi, :] = dot_nt(linv_ref[lo:hi, 0:hi], a_s[:, 0:hi])
    for t in range(W // step):
        lo, hi = t * step, (t + 1) * step
        r = dot_tn(linv_ref[lo:, lo:hi], f_s[lo:, :])
        high = r.astype(jnp.bfloat16)
        high_ref[lo:hi, :] = high
        low_ref[lo:hi, :] = (r - high.astype(F32)).astype(jnp.bfloat16)


def solve_across(y, linv):
    out = jax.ShapeDtypeStruct((W, 2 * B), jnp.bfloat16)
    spec = pl.BlockSpec((W, B), lambda q: (0, q))
    return pl.pallas_call(
        across_kernel,
        grid=(2,),
        in_specs=[
            pl.BlockSpec((N_ROW, N_COL, 1, 2, H, SL), lambda q: (0, 0, q, 0, 0, 0)),
            whole(),
        ],
        out_specs=[spec, spec],
        out_shape=[out, out],
        scratch_shapes=[VMEM((B, W), F32), VMEM((W, B), F32)],
        compiler_params=params(58),
        cost_estimate=cost(1.6e10, 12 * MIB),
        name="solve_across",
    )(y, linv)


STEP = 256


def product_kernel(x_ref, linv_ref, l_ref, high_ref, low_ref, p_ref, a_s):
    row = lax.axis_index("row")
    col = lax.axis_index("col")
    part = pl.program_id(0)
    front_row = row + N_ROW * part

    @pl.when(front_row >= 2)
    def _():
        for blk in range(2):
            gather_rows(a_s, 0, blk * B, lambda src, dev: x_ref[src, dev, 0, blk])
        f = a_s[...]
        f_high = f.astype(jnp.bfloat16)
        f_low = (f - f_high.astype(F32)).astype(jnp.bfloat16)

        def mul(x, y):
            return lax.dot_general(x, y, (((1,), (0,)), ((), ())), preferred_element_type=F32)

        def columns(start, stop):
            for lo in range(start, stop, STEP):
                ts = slice(lo, lo + STEP)
                high = high_ref[:, ts]
                p_ref[:, ts] = mul(f_high, high) + (mul(f_low, high) + mul(f_high, low_ref[:, ts]))

        columns(B, 2 * B)

        @pl.when(col >= 2)
        def _():
            columns(0, B)

        for panel in range(2):

            @pl.when(col == panel)
            def _():
                for lo in range(0, B, STEP):
                    at = panel * B + lo
                    p_ref[:, lo : lo + STEP] = -dot_nt(
                        a_s[:, : at + STEP], linv_ref[at : at + STEP, : at + STEP]
                    )

    @pl.when(front_row < 2)
    def _():
        p_ref[...] = jnp.zeros_like(p_ref)
        for panel in range(2):

            @pl.when(col == panel)
            def _():
                rows = pl.ds(pl.multiple_of(jnp.minimum(front_row, 1) * B, B), B)
                p_ref[:, 0:B] = -l_ref[rows, panel * B : (panel + 1) * B]


def panel_product(x, linv, lower, high, low):
    return pl.pallas_call(
        product_kernel,
        grid=(4,),
        in_specs=[
            pl.BlockSpec((N_COL, N_ROW, 1, 2, H, SL), lambda s: (0, 0, s, 0, 0, 0)),
            whole(),
            whole(),
            whole(),
            whole(),
        ],
        out_specs=pl.BlockSpec((B, 2 * B), lambda s: (s, 0)),
        out_shape=jax.ShapeDtypeStruct((4 * B, 2 * B), F32),
        scratch_shapes=[VMEM((B, W), F32)],
        compiler_params=params(58),
        cost_estimate=cost(2.5e10, 30 * MIB),
        name="panel_product",
    )(x, linv, lower, high, low)


def finish_kernel(recv_ref, p_ref, diag_ref, out_ref, tile_s):
    row = lax.axis_index("row")
    col = lax.axis_index("col")
    front_row = row + N_ROW * pl.program_id(0)
    front_col = col + N_COL * pl.program_id(1)
    inside = jnp.logical_and(front_row >= 2, front_col >= 2)

    @pl.when(jnp.logical_and(inside, front_row >= front_col))
    def _():
        for half in range(2):
            for js in range(4):
                cs = slice(js * SL, (js + 1) * SL)
                for src in range(N_COL):
                    lo = src * 2 * H + half * H
                    out_ref[lo : lo + H, cs] = (
                        recv_ref[half * 4 + js, src, 0, 0] - p_ref[lo : lo + H, cs]
                    )

    @pl.when(jnp.logical_and(inside, front_row < front_col))
    def _():
        for js in range(4):
            rs = slice(js * SL, (js + 1) * SL)
            for t in range(4):
                for src in range(4):
                    for half in range(2):
                        lo = src * 2 * H + half * H
                        tile_s[js, t, lo : lo + H, :] = recv_ref[half * 4 + js, t * 4 + src, 0, 0]
                ts = slice(t * SL, (t + 1) * SL)
                out_ref[rs, ts] = tile_s[js, t].T - p_ref[rs, ts]

    @pl.when(jnp.logical_not(inside))
    def _():
        out_ref[...] = -p_ref[...]

    @pl.when(jnp.logical_and(inside, front_row == front_col))
    def _():
        for t in range(B // SL):
            ts = slice(t * SL, (t + 1) * SL)
            eye = lax.broadcasted_iota(jnp.int32, (SL, SL), 0) == lax.broadcasted_iota(
                jnp.int32, (SL, SL), 1
            )
            d = diag_ref[front_row, :, ts]
            out_ref[ts, ts] = out_ref[ts, ts] + jnp.where(eye, d, 0.0)


def finish(received, product, diag):
    spec = pl.BlockSpec((B, B), lambda s, q: (s, q))
    return pl.pallas_call(
        finish_kernel,
        grid=(4, 2),
        in_specs=[
            pl.BlockSpec((N_ROW, N_COL, 1, 1, H, SL), lambda s, q: (0, 0, s, q, 0, 0)),
            spec,
            whole(),
        ],
        out_specs=spec,
        out_shape=jax.ShapeDtypeStruct((4 * B, 2 * B), F32),
        scratch_shapes=[VMEM((4, 4, SL, SL), F32)],
        compiler_params=params(58),
        cost_estimate=cost(0, 24 * MIB),
        name="finish",
    )(received, product, diag)


def swap(x):
    half_rows = N_ROW // 2
    return lax.ppermute(x, "row", [(i, (i + half_rows) % N_ROW) for i in range(N_ROW)])


def exchange(x, axes):
    return lax.all_to_all(x, axes, split_axis=0, concat_axis=0, tiled=True)


def shards(child_fronts, parent_diagonal, block_maps):
    child = child_fronts.transpose(0, 2, 1, 3)
    p_keep, p_send = split_panel(child)
    p_other = swap(p_send)
    r_keep, r_send = split_rest(child)
    r_other = swap(r_send)
    xd, y = panel_pieces(block_maps, p_keep, p_other)

    xd = exchange(xd, "row")
    d = lax.all_gather(xd[:, 8:], "col", axis=0, tiled=False)
    lower, inverse = cholesky(d, parent_diagonal[: 2 * B].reshape(1, 2 * B))
    x = lax.all_gather(xd[:, :8].reshape(N_ROW, 4, 2, H, SL), "col", axis=0, tiled=False)
    packed = pack(block_maps, p_keep, p_other, r_keep, r_other)
    y = lax.all_gather(exchange(y, "col"), "row", axis=0, tiled=False)

    received = exchange(packed.reshape(N_ROW * N_COL, 4, 2, H, SL), ("row", "col"))
    received = received.reshape(N_ROW, N_COL, 4, 2, H, SL)

    high, low = solve_across(y, inverse)
    product = panel_product(x, inverse, lower, high, low)
    return finish(received, product, parent_diagonal.reshape(NB, 1, B))


def solution(mesh):
    return jax.shard_map(
        shards,
        mesh=mesh,
        in_specs=(P(None, "col", None, "row"), P(), P()),
        out_specs=P("row", "col"),
        check_vma=False,
    )
```

```python
import functools

import jax
import jax.numpy as jnp
from jax import lax
from jax.experimental import pallas as pl
from jax.experimental.pallas import tpu as pltpu
from jax.sharding import PartitionSpec as P

B = 512
NB = 32
NCB = 20
N_ROW = 8
N_COL = 16
W = 2 * B
H = 16
SL = 128
CB = 128
ST = 16
HI = lax.Precision.HIGHEST
F32 = jnp.float32
BF16 = jnp.bfloat16
VMEM = pltpu.VMEM
MIB = 1024 * 1024


def whole():
    return pl.BlockSpec(memory_space=VMEM)


def smem():
    return pl.BlockSpec(memory_space=pltpu.SMEM)


def params(mib):
    return pltpu.CompilerParams(vmem_limit_bytes=mib * MIB)


def cost(flops, nbytes):
    return pl.CostEstimate(flops=int(flops), bytes_accessed=int(nbytes), transcendentals=0)


def invert_maps(maps_ref, inv_ref):
    def clear(i, _):
        inv_ref[0, i] = NCB
        inv_ref[1, i] = NCB
        return 0

    lax.fori_loop(0, NB, clear, 0)

    def fill(b, _):
        inv_ref[0, maps_ref[0, b]] = b
        inv_ref[1, maps_ref[1, b]] = b
        return 0

    lax.fori_loop(0, NCB, fill, 0)


TRI = (NCB - 1) * (NCB - 2) // 2


def split_panel_kernel(child_ref, keep_ref, send_ref):
    half = lax.axis_index("row") // (N_ROW // 2)
    keep = pl.ds(pl.multiple_of(half * H, H), H)
    send = pl.ds(pl.multiple_of((1 - half) * H, H), H)
    for b in range(2):
        keep_ref[b] = child_ref[:, b, keep]
        send_ref[b] = child_ref[:, b, send]


def split_panel(child):
    shape = jax.ShapeDtypeStruct((2, NCB, H, SL), F32)
    return pl.pallas_call(
        split_panel_kernel,
        grid=(1,),
        in_specs=[pl.BlockSpec((NCB, 2, 2 * H, SL), lambda g: (0, 0, 0, 0))],
        out_specs=[whole(), whole()],
        out_shape=[shape, shape],
        compiler_params=params(58),
        cost_estimate=cost(0, 2 * MIB),
        name="split_panel",
    )(child)


def split_rest_kernel(child_ref, keep_ref, send_ref):
    half = lax.axis_index("row") // (N_ROW // 2)
    keep = pl.ds(pl.multiple_of(half * H, H), H)
    send = pl.ds(pl.multiple_of((1 - half) * H, H), H)
    for a in range(2, NCB):
        at = (a - 1) * (a - 2) // 2
        keep_ref[at : at + a - 1] = child_ref[a, 2 : a + 1, keep]
        send_ref[at : at + a - 1] = child_ref[a, 2 : a + 1, send]


def split_rest(child):
    shape = jax.ShapeDtypeStruct((TRI, H, SL), F32)
    return pl.pallas_call(
        split_rest_kernel,
        in_specs=[whole()],
        out_specs=[whole(), whole()],
        out_shape=[shape, shape],
        compiler_params=params(58),
        cost_estimate=cost(0, 10 * MIB),
        name="split_rest",
    )(child)


def panel_kernel(maps_ref, keep_ref, other_ref, xd_ref, y_ref, sum_ref, inv_ref):
    child = lax.axis_index("row") // (N_ROW // 2)
    invert_maps(maps_ref, inv_ref)

    def tile(ref, c, i, blk):
        a = inv_ref[c, i]
        b = inv_ref[c, blk]
        ok = jnp.maximum(a, b) < NCB
        return jnp.where(ok, ref[jnp.minimum(b, 1), jnp.minimum(a, NCB - 1)], 0.0)

    def collect(i, _):
        for blk in range(2):
            sum_ref[blk, i] = tile(keep_ref, child, i, blk) + tile(other_ref, 1 - child, i, blk)
        return 0

    lax.fori_loop(0, NB, collect, 0)
    for row in range(N_ROW):
        for part in range(4):
            for blk in range(2):
                xd_ref[row, part * 2 + blk] = sum_ref[blk, row + N_ROW * part]
        for at, (blk, other) in enumerate(((0, 0), (0, 1), (1, 1))):
            xd_ref[row, 8 + at] = sum_ref[other, blk]
    for col in range(N_COL):
        for side in range(2):
            for blk in range(2):
                y_ref[col, side, blk] = sum_ref[blk, col + N_COL * side]


def panel_pieces(maps, keep, other):
    return pl.pallas_call(
        panel_kernel,
        in_specs=[smem(), whole(), whole()],
        out_specs=[whole(), whole()],
        out_shape=[
            jax.ShapeDtypeStruct((N_ROW, 11, H, SL), F32),
            jax.ShapeDtypeStruct((N_COL, 2, 2, H, SL), F32),
        ],
        scratch_shapes=[VMEM((2, NB, H, SL), F32), pltpu.SMEM((2, NB), jnp.int32)],
        compiler_params=params(58),
        cost_estimate=cost(0, 3 * MIB),
        name="panel_pieces",
    )(maps, keep, other)


WIDE = NCB + 1


def pack_kernel(maps_ref, p0_ref, p1_ref, r0_ref, r1_ref, out_ref, t0_ref, t1_ref, inv_ref):
    child = lax.axis_index("row") // (N_ROW // 2)
    row = pl.program_id(0)

    @pl.when(row == 0)
    def _():
        invert_maps(maps_ref, inv_ref)
        for p_ref, r_ref, t_ref in ((p0_ref, r0_ref, t0_ref), (p1_ref, r1_ref, t1_ref)):
            for a in range(NCB):
                for b in range(min(a + 1, 2)):
                    t_ref[a * WIDE + b] = p_ref[b, a]
                if a >= 2:
                    at = (a - 1) * (a - 2) // 2
                    t_ref[a * WIDE + 2 : a * WIDE + a + 1] = r_ref[at : at + a - 1]
            t_ref[NCB * WIDE : WIDE * WIDE] = jnp.zeros((WIDE, H, SL), F32)

    rows = [
        (inv_ref[child, row + N_ROW * part], inv_ref[1 - child, row + N_ROW * part])
        for part in range(4)
    ]

    def across(col, _):
        for side in range(2):
            j0 = inv_ref[child, col + N_COL * side]
            j1 = inv_ref[1 - child, col + N_COL * side]
            for part in range(4):
                i0, i1 = rows[part]
                out_ref[0, col, part, side] = (
                    t0_ref[jnp.maximum(i0, j0) * WIDE + jnp.minimum(i0, j0)]
                    + t1_ref[jnp.maximum(i1, j1) * WIDE + jnp.minimum(i1, j1)]
                )
        return 0

    lax.fori_loop(0, N_COL, across, 0, unroll=2)


def pack(maps, p0, p1, r0, r1):
    return pl.pallas_call(
        pack_kernel,
        grid=(N_ROW,),
        in_specs=[smem(), whole(), whole(), whole(), whole()],
        out_specs=pl.BlockSpec((1, N_COL, 4, 2, H, SL), lambda r: (r, 0, 0, 0, 0, 0)),
        out_shape=jax.ShapeDtypeStruct((N_ROW, N_COL, 4, 2, H, SL), F32),
        scratch_shapes=[
            VMEM((WIDE * WIDE, H, SL), F32),
            VMEM((WIDE * WIDE, H, SL), F32),
            pltpu.SMEM((2, NB), jnp.int32),
        ],
        compiler_params=params(58),
        cost_estimate=cost(0, 16 * MIB),
        name="pack",
    )(maps, p0, p1, r0, r1)


def dot_tn(a, b):
    return lax.dot_general(a, b, (((0,), (0,)), ((), ())), precision=HI, preferred_element_type=F32)


def dot_nn(a, b):
    return lax.dot_general(a, b, (((1,), (0,)), ((), ())), precision=HI, preferred_element_type=F32)


def dot_nt(a, b):
    return lax.dot_general(a, b, (((1,), (1,)), ((), ())), precision=HI, preferred_element_type=F32)


def split(x, high_ref, low_ref, rows, cols=slice(None)):
    high = x.astype(BF16)
    high_ref[rows, cols] = high
    low_ref[rows, cols] = (x - high.astype(F32)).astype(BF16)


def dot3(a_high, a_low, b_high, b_low, dims):
    def mul(x, y):
        return lax.dot_general(x, y, (dims, ((), ())), preferred_element_type=F32)

    return mul(a_high, b_high) + (mul(a_low, b_high) + mul(a_high, b_low))


def factor_block(t_ref, w_ref, s_ref, e_ref):
    for p in range(CB // ST):
        lo = p * ST
        rows = lax.broadcasted_iota(jnp.int32, (ST, CB), 0)
        cols = lax.broadcasted_iota(jnp.int32, (ST, CB), 1)
        ident = jnp.where(cols == rows + lo, 1.0, 0.0).astype(F32)
        s = jnp.concatenate([t_ref[lo : lo + ST, :], ident], axis=1)
        if p:
            s = s - dot_tn(w_ref[0:lo, lo : lo + ST], w_ref[0:lo, :])
        s_ref[...] = s
        for c in range(ST):
            e_ref[c] = jnp.broadcast_to(s[:, lo + c : lo + c + 1], (ST, CB))
        e = {}
        for c in range(ST):
            for r in range(c, ST):
                e[r, c] = e_ref[c, r : r + 1, :]
        done = []
        for j in range(ST):
            inv = lax.rsqrt(e[j, j])
            for r in range(j + 1, ST):
                e[r, j] = e[r, j] * inv
            for c in range(j + 1, ST):
                for r in range(c, ST):
                    e[r, c] = e[r, c] - e[r, j] * e[c, j]
            u = s_ref[j : j + 1, :]
            for m in range(j):
                u = u - jnp.concatenate([e[j, m], e[j, m]], axis=1) * done[m]
            u = u * jnp.concatenate([inv, inv], axis=1)
            done.append(u)
            w_ref[lo + j : lo + j + 1, :] = u


def gather_rows(a_s, row, col, piece):
    for src in range(N_COL):
        for dev in range(N_ROW):
            lo = row + src * 2 * H + (dev // 4) * H
            at = col + (dev % 4) * SL
            a_s[lo : lo + H, at : at + SL] = piece(src, dev)


DB = 2 * CB
SIDE = 4
SHIFTS = (0, 3, 1, 2)


def chol_kernel(
    d0_ref, d1_ref, d2_ref, d3_ref, d4_ref, diag_ref, l_ref, linv_ref, high_ref, low_ref, a_s, w_s, s_s, e_s, t_s
):
    nb = W // DB
    me = lax.axis_index("col")
    halves = ((0, d0_ref, 0, 4), (3, d1_ref, 0, 4), (1, d2_ref, 0, 4), (2, d3_ref, 0, 2), (2, d4_ref, 2, 4))
    for zone, d_ref, first_x, stop_x in halves:
        for at_x in range(first_x, stop_x):
            shift = SHIFTS[at_x]
            src = lax.rem(me // SIDE + zone, SIDE) * SIDE + lax.rem(lax.rem(me, SIDE) + shift, SIDE)
            for half in range(2):
                first = src * 2 * H + half * H
                for js in range(4):
                    for at, (blk, other) in enumerate(((0, 0), (0, 1), (1, 1))):
                        rows = pl.ds(pl.multiple_of(blk * B + first, H), H)
                        lo = other * B + js * SL
                        a_s[rows, lo : lo + SL] = d_ref[at_x - first_x, half * 4 + js, at]
    low = lax.broadcasted_iota(jnp.int32, (CB, CB), 0)
    high = lax.broadcasted_iota(jnp.int32, (CB, CB), 1)
    l_ref[...] = jnp.zeros_like(l_ref)
    linv_ref[...] = jnp.zeros_like(linv_ref)
    for t in range(W // CB):
        ts = slice(t * CB, (t + 1) * CB)
        a_s[ts, ts] = a_s[ts, ts] + jnp.where(low == high, diag_ref[0:1, ts], 0.0)

    def block(i):
        return pl.ds(pl.multiple_of(i * DB, DB), DB)

    def factor():
        factor_block(t_s, w_s, s_s, e_s)
        return jnp.where(low <= high, w_s[:, :CB], 0.0), jnp.where(low >= high, w_s[:, CB:], 0.0)

    def step(k, _):
        ks = block(k)
        k0 = pl.ds(pl.multiple_of(k * DB, CB), CB)
        k1 = pl.ds(pl.multiple_of(k * DB + CB, CB), CB)
        t_s[...] = a_s[k0, k0]
        upper, inverse = factor()
        l_ref[k0, k0] = upper.T
        linv_ref[k0, k0] = inverse
        right = dot_nn(inverse, a_s[k0, k1])
        l_ref[k1, k0] = right.T
        t_s[...] = a_s[k1, k1] - dot_tn(right, right)
        between = dot_tn(right, inverse)
        upper, inverse = factor()
        l_ref[k1, k1] = upper.T
        linv_ref[k1, k1] = inverse
        linv_ref[k1, k0] = -dot_nn(inverse, between)

        def solve(j, _):
            js = block(j)
            r = dot_nn(linv_ref[ks, ks], a_s[ks, js])
            a_s[ks, js] = r
            l_ref[js, ks] = r.T
            return 0

        lax.fori_loop(k + 1, nb, solve, 0)

        def update(i, _):
            ins = block(i)

            def inner(j, _):
                js = block(j)
                a_s[ins, js] = a_s[ins, js] - dot_tn(a_s[ks, ins], a_s[ks, js])
                return 0

            lax.fori_loop(i, nb, inner, 0)
            return 0

        lax.fori_loop(k + 1, nb, update, 0)
        return 0

    lax.fori_loop(0, nb, step, 0)
    for i in range(1, nb):
        lo = i * DB
        acc = dot_nn(l_ref[lo : lo + DB, 0:lo], linv_ref[0:lo, 0:lo])
        linv_ref[lo : lo + DB, 0:lo] = -dot_nn(linv_ref[lo : lo + DB, lo : lo + DB], acc)
    for lo in range(0, W, DB):
        split(dot_tn(linv_ref[lo:, lo : lo + DB], linv_ref[lo:, :]), high_ref, low_ref, slice(lo, lo + DB))


def cholesky(pieces, diag):
    return pl.pallas_call(
        chol_kernel,
        in_specs=[whole()] * 6,
        out_specs=[whole()] * 4,
        out_shape=[jax.ShapeDtypeStruct((W, W), t) for t in (F32, F32, BF16, BF16)],
        scratch_shapes=[
            VMEM((W, W), F32),
            VMEM((CB, 2 * CB), F32),
            VMEM((ST, 2 * CB), F32),
            VMEM((ST, ST, CB), F32),
            VMEM((CB, CB), F32),
        ],
        compiler_params=params(58),
        cost_estimate=cost(5e10, 12 * MIB),
        name="leading_cholesky",
    )(*pieces, diag)


STEP = 256


def rows_kernel(x_ref, linv_ref, l_ref, kh_ref, kl_ref, high_ref, low_ref, panel_ref, a_s):
    row = lax.axis_index("row")
    col = lax.axis_index("col")
    front_row = row + N_ROW * pl.program_id(0)

    @pl.when(front_row >= 2)
    def _():
        for blk in range(2):
            gather_rows(a_s, 0, blk * B, lambda src, dev: x_ref[src, dev, 0, blk])
        a = a_s[...]
        a_high = a.astype(BF16)
        a_low = (a - a_high.astype(F32)).astype(BF16)
        for lo in range(0, W, STEP):
            ts = slice(lo, lo + STEP)
            n = dot3(a_high, a_low, kh_ref[:, ts], kl_ref[:, ts], ((1,), (0,)))
            split(n, high_ref, low_ref, slice(None), ts)
        for panel in range(2):

            @pl.when(col == panel)
            def _():
                for lo in range(0, B, STEP):
                    at = panel * B + lo
                    panel_ref[:, lo : lo + STEP] = dot_nt(
                        a_s[:, : at + STEP], linv_ref[at : at + STEP, : at + STEP]
                    )

    @pl.when(front_row < 2)
    def _():
        for panel in range(2):

            @pl.when(col == panel)
            def _():
                rows = pl.ds(pl.multiple_of(jnp.minimum(front_row, 1) * B, B), B)
                panel_ref[...] = l_ref[rows, panel * B : (panel + 1) * B]


def solve_rows(x, inverse, lower, high, low):
    spec = pl.BlockSpec((B, W), lambda s: (s, 0))
    return pl.pallas_call(
        rows_kernel,
        grid=(4,),
        in_specs=[pl.BlockSpec((N_COL, N_ROW, 1, 2, H, SL), lambda s: (0, 0, s, 0, 0, 0))]
        + [whole()] * 4,
        out_specs=[spec, spec, pl.BlockSpec((B, B), lambda s: (s, 0))],
        out_shape=[
            jax.ShapeDtypeStruct((4 * B, W), BF16),
            jax.ShapeDtypeStruct((4 * B, W), BF16),
            jax.ShapeDtypeStruct((4 * B, B), F32),
        ],
        scratch_shapes=[VMEM((B, W), F32)],
        compiler_params=params(58),
        cost_estimate=cost(1.5e10, 30 * MIB),
        name="solve_rows",
    )(x, inverse, lower, high, low)


def finish_kernel(
    recv_ref, nh_ref, nl_ref, y_ref, panel_ref, diag_ref, out_ref, p_s, tile_s, yh_s, yl_s
):
    side = pl.program_id(0)
    part = pl.program_id(1)
    front_row = lax.axis_index("row") + N_ROW * part
    front_col = lax.axis_index("col") + N_COL * side
    inside = jnp.logical_and(front_row >= 2, front_col >= 2)

    @pl.when(part == 0)
    def _():
        for blk in range(2):
            for src in range(N_COL):
                for dev in range(N_ROW):
                    lo = src * 2 * H + (dev // 4) * H
                    at = blk * B + (dev % 4) * SL
                    split(
                        y_ref[dev, src, 0, blk], yh_s, yl_s, slice(lo, lo + H), slice(at, at + SL)
                    )

    @pl.when(inside)
    def _():
        for lo in range(0, B, STEP):
            ts = slice(lo, lo + STEP)
            p_s[:, ts] = dot3(nh_ref[...], nl_ref[...], yh_s[ts, :], yl_s[ts, :], ((1,), (1,)))

    @pl.when(jnp.logical_and(inside, front_row >= front_col))
    def _():
        for dev in range(N_ROW):
            cs = slice((dev % 4) * SL, (dev % 4 + 1) * SL)
            for src in range(N_COL):
                lo = src * 2 * H + (dev // 4) * H
                out_ref[lo : lo + H, cs] = recv_ref[dev, src, 0, 0] - p_s[lo : lo + H, cs]

    @pl.when(jnp.logical_and(inside, front_row < front_col))
    def _():
        for js in range(4):
            rs = slice(js * SL, (js + 1) * SL)
            for t in range(4):
                for src in range(4):
                    for half in range(2):
                        lo = src * 2 * H + half * H
                        tile_s[js, t, lo : lo + H, :] = recv_ref[half * 4 + js, t * 4 + src, 0, 0]
                ts = slice(t * SL, (t + 1) * SL)
                out_ref[rs, ts] = tile_s[js, t].T - p_s[rs, ts]

    @pl.when(front_col < 2)
    def _():
        out_ref[...] = panel_ref[...]

    @pl.when(jnp.logical_and(front_row < 2, front_col >= 2))
    def _():
        out_ref[...] = jnp.zeros_like(out_ref)

    @pl.when(jnp.logical_and(inside, front_row == front_col))
    def _():
        for t in range(B // SL):
            ts = slice(t * SL, (t + 1) * SL)
            eye = lax.broadcasted_iota(jnp.int32, (SL, SL), 0) == lax.broadcasted_iota(
                jnp.int32, (SL, SL), 1
            )
            d = diag_ref[front_row, :, ts]
            out_ref[ts, ts] = out_ref[ts, ts] + jnp.where(eye, d, 0.0)


def finish(received, high, low, y, panel, diag):
    rows = pl.BlockSpec((B, W), lambda q, s: (s, 0))
    return pl.pallas_call(
        finish_kernel,
        grid=(2, 4),
        in_specs=[
            pl.BlockSpec((N_ROW, N_COL, 1, 1, H, SL), lambda q, s: (0, 0, s, q, 0, 0)),
            rows,
            rows,
            pl.BlockSpec((N_ROW, N_COL, 1, 2, H, SL), lambda q, s: (0, 0, q, 0, 0, 0)),
            pl.BlockSpec((B, B), lambda q, s: (s * (1 - q), 0)),
            whole(),
        ],
        out_specs=pl.BlockSpec((B, B), lambda q, s: (s, q)),
        out_shape=jax.ShapeDtypeStruct((4 * B, 2 * B), F32),
        scratch_shapes=[
            VMEM((B, B), F32),
            VMEM((4, 4, SL, SL), F32),
            VMEM((B, W), BF16),
            VMEM((B, W), BF16),
        ],
        compiler_params=params(58),
        cost_estimate=cost(1.3e10, 30 * MIB),
        name="finish",
    )(received, high, low, y, panel, diag)


def swap(x):
    half_rows = N_ROW // 2
    return lax.ppermute(x, "row", [(i, (i + half_rows) % N_ROW) for i in range(N_ROW)])


def exchange(x, axes):
    return lax.all_to_all(x, axes, split_axis=0, concat_axis=0, tiled=True)


def from_shift(x, stride, shift):
    pairs = []
    for i in range(N_COL):
        place = (i // stride) % SIDE
        target = (place - shift) % SIDE
        pairs.append((i, i + (target - place) * stride))
    return lax.ppermute(x, "col", pairs)


def shards(child_fronts, parent_diagonal, block_maps):
    child = child_fronts.transpose(0, 2, 1, 3)
    p_keep, p_send = split_panel(child)
    p_other = swap(p_send)
    r_keep, r_send = split_rest(child)
    r_other = swap(r_send)
    xd, y = panel_pieces(block_maps, p_keep, p_other)

    xd = exchange(xd, "row")
    x = lax.all_gather(xd[:, :8].reshape(N_ROW, 4, 2, H, SL), "col", axis=0, tiled=False)
    d = xd[:, 8:]
    d = jnp.stack([d] + [from_shift(d, 1, shift) for shift in SHIFTS[1:]])
    before, after = from_shift(d, SIDE, 3), from_shift(d, SIDE, 1)
    d = (d, before, after, from_shift(before[:2], SIDE, 3), from_shift(after[2:], SIDE, 1))
    packed = pack(block_maps, p_keep, p_other, r_keep, r_other)
    packed, *d = lax.optimization_barrier((packed, *d))
    lower, inverse, high, low = cholesky(d, parent_diagonal[: 2 * B].reshape(1, 2 * B))
    y, _ = lax.optimization_barrier((y, r_other))
    y = lax.all_gather(exchange(y, "col"), "row", axis=0, tiled=False)
    high, low, panel = solve_rows(x, inverse, lower, high, low)

    received = exchange(packed.reshape(N_ROW * N_COL, 4, 2, H, SL), ("row", "col"))
    received = received.reshape(N_ROW, N_COL, 4, 2, H, SL)

    return finish(received, high, low, y, panel, parent_diagonal.reshape(NB, 1, B))


def solution(mesh):
    return jax.shard_map(
        shards,
        mesh=mesh,
        in_specs=(P(None, "col", None, "row"), P(), P()),
        out_specs=P("row", "col"),
        check_vma=False,
    )
```

```python
import functools

import jax
import jax.numpy as jnp
from jax import lax
from jax.experimental import pallas as pl
from jax.experimental.pallas import tpu as pltpu
from jax.sharding import PartitionSpec as P

B = 512
NB = 32
NCB = 20
N_ROW = 8
N_COL = 16
W = 2 * B
H = 16
SL = 128
CB = 128
ST = 16
HI = lax.Precision.HIGHEST
F32 = jnp.float32
BF16 = jnp.bfloat16
VMEM = pltpu.VMEM
MIB = 1024 * 1024


def whole():
    return pl.BlockSpec(memory_space=VMEM)


def smem():
    return pl.BlockSpec(memory_space=pltpu.SMEM)


def params(mib):
    return pltpu.CompilerParams(vmem_limit_bytes=mib * MIB)


def cost(flops, nbytes):
    return pl.CostEstimate(flops=int(flops), bytes_accessed=int(nbytes), transcendentals=0)


def invert_maps(maps_ref, inv_ref):
    def clear(i, _):
        inv_ref[0, i] = NCB
        inv_ref[1, i] = NCB
        return 0

    lax.fori_loop(0, NB, clear, 0)

    def fill(b, _):
        inv_ref[0, maps_ref[0, b]] = b
        inv_ref[1, maps_ref[1, b]] = b
        return 0

    lax.fori_loop(0, NCB, fill, 0)


TRI = (NCB - 1) * (NCB - 2) // 2


def split_panel_kernel(child_ref, keep_ref, send_ref):
    half = lax.axis_index("row") // (N_ROW // 2)
    keep = pl.ds(pl.multiple_of(half * H, H), H)
    send = pl.ds(pl.multiple_of((1 - half) * H, H), H)
    for b in range(2):
        keep_ref[b] = child_ref[:, b, keep]
        send_ref[b] = child_ref[:, b, send]


def split_panel(child):
    shape = jax.ShapeDtypeStruct((2, NCB, H, SL), F32)
    return pl.pallas_call(
        split_panel_kernel,
        grid=(1,),
        in_specs=[pl.BlockSpec((NCB, 2, 2 * H, SL), lambda g: (0, 0, 0, 0))],
        out_specs=[whole(), whole()],
        out_shape=[shape, shape],
        compiler_params=params(58),
        cost_estimate=cost(0, 2 * MIB),
        name="split_panel",
    )(child)


def split_rest_kernel(child_ref, keep_ref, send_ref):
    half = lax.axis_index("row") // (N_ROW // 2)
    keep = pl.ds(pl.multiple_of(half * H, H), H)
    send = pl.ds(pl.multiple_of((1 - half) * H, H), H)
    for a in range(2, NCB):
        at = (a - 1) * (a - 2) // 2
        keep_ref[at : at + a - 1] = child_ref[a, 2 : a + 1, keep]
        send_ref[at : at + a - 1] = child_ref[a, 2 : a + 1, send]


def split_rest(child):
    shape = jax.ShapeDtypeStruct((TRI, H, SL), F32)
    return pl.pallas_call(
        split_rest_kernel,
        in_specs=[whole()],
        out_specs=[whole(), whole()],
        out_shape=[shape, shape],
        compiler_params=params(58),
        cost_estimate=cost(0, 10 * MIB),
        name="split_rest",
    )(child)


def panel_kernel(maps_ref, keep_ref, other_ref, xd_ref, y_ref, sum_ref, inv_ref):
    child = lax.axis_index("row") // (N_ROW // 2)
    invert_maps(maps_ref, inv_ref)

    def tile(ref, c, i, blk):
        a = inv_ref[c, i]
        b = inv_ref[c, blk]
        ok = jnp.maximum(a, b) < NCB
        return jnp.where(ok, ref[jnp.minimum(b, 1), jnp.minimum(a, NCB - 1)], 0.0)

    def collect(i, _):
        for blk in range(2):
            sum_ref[blk, i] = tile(keep_ref, child, i, blk) + tile(other_ref, 1 - child, i, blk)
        return 0

    lax.fori_loop(0, NB, collect, 0)
    for row in range(N_ROW):
        for part in range(4):
            for blk in range(2):
                xd_ref[row, part * 2 + blk] = sum_ref[blk, row + N_ROW * part]
        for at, (blk, other) in enumerate(((0, 0), (0, 1), (1, 1))):
            xd_ref[row, 8 + at] = sum_ref[other, blk]
    for col in range(N_COL):
        for side in range(2):
            for blk in range(2):
                y_ref[col, side, blk] = sum_ref[blk, col + N_COL * side]


def panel_pieces(maps, keep, other):
    return pl.pallas_call(
        panel_kernel,
        in_specs=[smem(), whole(), whole()],
        out_specs=[whole(), whole()],
        out_shape=[
            jax.ShapeDtypeStruct((N_ROW, 11, H, SL), F32),
            jax.ShapeDtypeStruct((N_COL, 2, 2, H, SL), F32),
        ],
        scratch_shapes=[VMEM((2, NB, H, SL), F32), pltpu.SMEM((2, NB), jnp.int32)],
        compiler_params=params(58),
        cost_estimate=cost(0, 3 * MIB),
        name="panel_pieces",
    )(maps, keep, other)


WIDE = NCB + 1


def pack_kernel(maps_ref, p0_ref, p1_ref, r0_ref, r1_ref, out_ref, t0_ref, t1_ref, inv_ref):
    child = lax.axis_index("row") // (N_ROW // 2)
    row = pl.program_id(0)

    @pl.when(row == 0)
    def _():
        invert_maps(maps_ref, inv_ref)
        for p_ref, r_ref, t_ref in ((p0_ref, r0_ref, t0_ref), (p1_ref, r1_ref, t1_ref)):
            for a in range(NCB):
                for b in range(min(a + 1, 2)):
                    t_ref[a * WIDE + b] = p_ref[b, a]
                if a >= 2:
                    at = (a - 1) * (a - 2) // 2
                    t_ref[a * WIDE + 2 : a * WIDE + a + 1] = r_ref[at : at + a - 1]
            t_ref[NCB * WIDE : WIDE * WIDE] = jnp.zeros((WIDE, H, SL), F32)

    rows = [
        (inv_ref[child, row + N_ROW * part], inv_ref[1 - child, row + N_ROW * part])
        for part in range(4)
    ]

    def across(col, _):
        for side in range(2):
            j0 = inv_ref[child, col + N_COL * side]
            j1 = inv_ref[1 - child, col + N_COL * side]
            for part in range(4):
                i0, i1 = rows[part]
                out_ref[0, col, part, side] = (
                    t0_ref[jnp.maximum(i0, j0) * WIDE + jnp.minimum(i0, j0)]
                    + t1_ref[jnp.maximum(i1, j1) * WIDE + jnp.minimum(i1, j1)]
                )
        return 0

    lax.fori_loop(0, N_COL, across, 0, unroll=2)


def pack(maps, p0, p1, r0, r1):
    return pl.pallas_call(
        pack_kernel,
        grid=(N_ROW,),
        in_specs=[smem(), whole(), whole(), whole(), whole()],
        out_specs=pl.BlockSpec((1, N_COL, 4, 2, H, SL), lambda r: (r, 0, 0, 0, 0, 0)),
        out_shape=jax.ShapeDtypeStruct((N_ROW, N_COL, 4, 2, H, SL), F32),
        scratch_shapes=[
            VMEM((WIDE * WIDE, H, SL), F32),
            VMEM((WIDE * WIDE, H, SL), F32),
            pltpu.SMEM((2, NB), jnp.int32),
        ],
        compiler_params=params(58),
        cost_estimate=cost(0, 16 * MIB),
        name="pack",
    )(maps, p0, p1, r0, r1)


def dot_tn(a, b):
    return lax.dot_general(a, b, (((0,), (0,)), ((), ())), precision=HI, preferred_element_type=F32)


def dot_nn(a, b):
    return lax.dot_general(a, b, (((1,), (0,)), ((), ())), precision=HI, preferred_element_type=F32)


def dot_nt(a, b):
    return lax.dot_general(a, b, (((1,), (1,)), ((), ())), precision=HI, preferred_element_type=F32)


def split(x, high_ref, low_ref, rows, cols=slice(None)):
    high = x.astype(BF16)
    high_ref[rows, cols] = high
    low_ref[rows, cols] = (x - high.astype(F32)).astype(BF16)


def dot3(a_high, a_low, b_high, b_low, dims):
    def mul(x, y):
        return lax.dot_general(x, y, (dims, ((), ())), preferred_element_type=F32)

    return mul(a_high, b_high) + (mul(a_low, b_high) + mul(a_high, b_low))


def factor_block(t_ref, w_ref, s_ref, e_ref):
    for p in range(CB // ST):
        lo = p * ST
        rows = lax.broadcasted_iota(jnp.int32, (ST, CB), 0)
        cols = lax.broadcasted_iota(jnp.int32, (ST, CB), 1)
        ident = jnp.where(cols == rows + lo, 1.0, 0.0).astype(F32)
        s = jnp.concatenate([t_ref[lo : lo + ST, :], ident], axis=1)
        if p:
            s = s - dot_tn(w_ref[0:lo, lo : lo + ST], w_ref[0:lo, :])
        s_ref[...] = s
        for c in range(ST):
            e_ref[c] = jnp.broadcast_to(s[:, lo + c : lo + c + 1], (ST, CB))
        e = {}
        for c in range(ST):
            for r in range(c, ST):
                e[r, c] = e_ref[c, r : r + 1, :]
        done = []
        for j in range(ST):
            inv = lax.rsqrt(e[j, j])
            for r in range(j + 1, ST):
                e[r, j] = e[r, j] * inv
            for c in range(j + 1, ST):
                for r in range(c, ST):
                    e[r, c] = e[r, c] - e[r, j] * e[c, j]
            u = s_ref[j : j + 1, :]
            for m in range(j):
                u = u - jnp.concatenate([e[j, m], e[j, m]], axis=1) * done[m]
            u = u * jnp.concatenate([inv, inv], axis=1)
            done.append(u)
            w_ref[lo + j : lo + j + 1, :] = u


def gather_rows(a_s, row, col, piece):
    for src in range(N_COL):
        for dev in range(N_ROW):
            lo = row + src * 2 * H + (dev // 4) * H
            at = col + (dev % 4) * SL
            a_s[lo : lo + H, at : at + SL] = piece(src, dev)


DB = 2 * CB
SIDE = 4
SHIFTS = (0, 3, 1, 2)


def chol_kernel(
    d0_ref, d1_ref, d2_ref, d3_ref, d4_ref, diag_ref, l_ref, linv_ref, high_ref, low_ref, a_s, w_s, s_s, e_s, t_s
):
    nb = W // DB
    me = lax.axis_index("col")
    halves = ((0, d0_ref, 0, 4), (3, d1_ref, 0, 4), (1, d2_ref, 0, 4), (2, d3_ref, 0, 2), (2, d4_ref, 2, 4))
    for zone, d_ref, first_x, stop_x in halves:
        for at_x in range(first_x, stop_x):
            shift = SHIFTS[at_x]
            src = lax.rem(me // SIDE + zone, SIDE) * SIDE + lax.rem(lax.rem(me, SIDE) + shift, SIDE)
            for half in range(2):
                first = src * 2 * H + half * H
                for js in range(4):
                    for at, (blk, other) in enumerate(((0, 0), (0, 1), (1, 1))):
                        rows = pl.ds(pl.multiple_of(blk * B + first, H), H)
                        lo = other * B + js * SL
                        a_s[rows, lo : lo + SL] = d_ref[at_x - first_x, half * 4 + js, at]
    low = lax.broadcasted_iota(jnp.int32, (CB, CB), 0)
    high = lax.broadcasted_iota(jnp.int32, (CB, CB), 1)
    l_ref[...] = jnp.zeros_like(l_ref)
    linv_ref[...] = jnp.zeros_like(linv_ref)
    for t in range(W // CB):
        ts = slice(t * CB, (t + 1) * CB)
        a_s[ts, ts] = a_s[ts, ts] + jnp.where(low == high, diag_ref[0:1, ts], 0.0)

    def block(i):
        return pl.ds(pl.multiple_of(i * DB, DB), DB)

    def factor():
        factor_block(t_s, w_s, s_s, e_s)
        return jnp.where(low <= high, w_s[:, :CB], 0.0), jnp.where(low >= high, w_s[:, CB:], 0.0)

    def step(k, _):
        ks = block(k)
        k0 = pl.ds(pl.multiple_of(k * DB, CB), CB)
        k1 = pl.ds(pl.multiple_of(k * DB + CB, CB), CB)
        t_s[...] = a_s[k0, k0]
        upper, inverse = factor()
        l_ref[k0, k0] = upper.T
        linv_ref[k0, k0] = inverse
        right = dot_nn(inverse, a_s[k0, k1])
        l_ref[k1, k0] = right.T
        t_s[...] = a_s[k1, k1] - dot_tn(right, right)
        between = dot_tn(right, inverse)
        upper, inverse = factor()
        l_ref[k1, k1] = upper.T
        linv_ref[k1, k1] = inverse
        linv_ref[k1, k0] = -dot_nn(inverse, between)

        def solve(j, _):
            js = block(j)
            r = dot_nn(linv_ref[ks, ks], a_s[ks, js])
            a_s[ks, js] = r
            l_ref[js, ks] = r.T
            return 0

        lax.fori_loop(k + 1, nb, solve, 0)

        def update(i, _):
            ins = block(i)

            def inner(j, _):
                js = block(j)
                a_s[ins, js] = a_s[ins, js] - dot_tn(a_s[ks, ins], a_s[ks, js])
                return 0

            lax.fori_loop(i, nb, inner, 0)
            return 0

        lax.fori_loop(k + 1, nb, update, 0)
        return 0

    lax.fori_loop(0, nb, step, 0)
    for i in range(1, nb):
        lo = i * DB
        acc = dot_nn(l_ref[lo : lo + DB, 0:lo], linv_ref[0:lo, 0:lo])
        linv_ref[lo : lo + DB, 0:lo] = -dot_nn(linv_ref[lo : lo + DB, lo : lo + DB], acc)
    for lo in range(0, W, DB):
        split(dot_tn(linv_ref[lo:, lo : lo + DB], linv_ref[lo:, :]), high_ref, low_ref, slice(lo, lo + DB))


def cholesky(pieces, diag):
    return pl.pallas_call(
        chol_kernel,
        in_specs=[whole()] * 6,
        out_specs=[whole()] * 4,
        out_shape=[jax.ShapeDtypeStruct((W, W), t) for t in (F32, F32, BF16, BF16)],
        scratch_shapes=[
            VMEM((W, W), F32),
            VMEM((CB, 2 * CB), F32),
            VMEM((ST, 2 * CB), F32),
            VMEM((ST, ST, CB), F32),
            VMEM((CB, CB), F32),
        ],
        compiler_params=params(58),
        cost_estimate=cost(5e10, 12 * MIB),
        name="leading_cholesky",
    )(*pieces, diag)


STEP = 256


def rows_kernel(x_ref, linv_ref, l_ref, kh_ref, kl_ref, high_ref, low_ref, panel_ref, a_s):
    row = lax.axis_index("row")
    col = lax.axis_index("col")
    front_row = row + N_ROW * pl.program_id(0)

    @pl.when(front_row >= 2)
    def _():
        for blk in range(2):
            gather_rows(a_s, 0, blk * B, lambda src, dev: x_ref[src, dev, 0, blk])
        a = a_s[...]
        a_high = a.astype(BF16)
        a_low = (a - a_high.astype(F32)).astype(BF16)
        for lo in range(0, W, STEP):
            ts = slice(lo, lo + STEP)
            n = dot3(a_high, a_low, kh_ref[:, ts], kl_ref[:, ts], ((1,), (0,)))
            split(n, high_ref, low_ref, slice(None), ts)
        for panel in range(2):

            @pl.when(col == panel)
            def _():
                for lo in range(0, B, STEP):
                    at = panel * B + lo
                    panel_ref[:, lo : lo + STEP] = dot_nt(
                        a_s[:, : at + STEP], linv_ref[at : at + STEP, : at + STEP]
                    )

    @pl.when(front_row < 2)
    def _():
        for panel in range(2):

            @pl.when(col == panel)
            def _():
                rows = pl.ds(pl.multiple_of(jnp.minimum(front_row, 1) * B, B), B)
                panel_ref[...] = l_ref[rows, panel * B : (panel + 1) * B]


def solve_rows(x, inverse, lower, high, low):
    spec = pl.BlockSpec((B, W), lambda s: (s, 0))
    return pl.pallas_call(
        rows_kernel,
        grid=(4,),
        in_specs=[pl.BlockSpec((N_COL, N_ROW, 1, 2, H, SL), lambda s: (0, 0, s, 0, 0, 0))]
        + [whole()] * 4,
        out_specs=[spec, spec, pl.BlockSpec((B, B), lambda s: (s, 0))],
        out_shape=[
            jax.ShapeDtypeStruct((4 * B, W), BF16),
            jax.ShapeDtypeStruct((4 * B, W), BF16),
            jax.ShapeDtypeStruct((4 * B, B), F32),
        ],
        scratch_shapes=[VMEM((B, W), F32)],
        compiler_params=params(58),
        cost_estimate=cost(1.5e10, 30 * MIB),
        name="solve_rows",
    )(x, inverse, lower, high, low)


def finish_kernel(
    recv_ref, nh_ref, nl_ref, y0_ref, y1_ref, y2_ref, y3_ref, y4_ref, panel_ref, diag_ref, out_ref,
    p_s, tile_s, yh_s, yl_s,
):
    side = pl.program_id(0)
    part = pl.program_id(1)
    front_row = lax.axis_index("row") + N_ROW * part
    front_col = lax.axis_index("col") + N_COL * side
    inside = jnp.logical_and(front_row >= 2, front_col >= 2)

    @pl.when(part == 0)
    def _():
        me = lax.axis_index("row")
        places = (
            (0, y0_ref, 0, 0), (0, y0_ref, 1, 1), (3, y1_ref, 0, 0), (3, y1_ref, 1, 1),
            (1, y2_ref, 0, 0), (1, y2_ref, 1, 1), (2, y3_ref, 0, 0), (2, y4_ref, 0, 1),
        )
        for shift, y_ref, at, core in places:
            place = lax.rem(me // 2 + shift, SIDE)
            dev = place * 2 + lax.rem(me + core, 2)
            for blk in range(2):
                cols = pl.ds(pl.multiple_of(blk * B + lax.rem(dev, 4) * SL, SL), SL)
                for src in range(N_COL):
                    rows = pl.ds(pl.multiple_of(src * 2 * H + (dev // 4) * H, H), H)
                    split(y_ref[at, src, 0, blk], yh_s, yl_s, rows, cols)

    @pl.when(inside)
    def _():
        for lo in range(0, B, STEP):
            ts = slice(lo, lo + STEP)
            p_s[:, ts] = dot3(nh_ref[...], nl_ref[...], yh_s[ts, :], yl_s[ts, :], ((1,), (1,)))

    @pl.when(jnp.logical_and(inside, front_row >= front_col))
    def _():
        for dev in range(N_ROW):
            cs = slice((dev % 4) * SL, (dev % 4 + 1) * SL)
            for src in range(N_COL):
                lo = src * 2 * H + (dev // 4) * H
                out_ref[lo : lo + H, cs] = recv_ref[dev, src, 0, 0] - p_s[lo : lo + H, cs]

    @pl.when(jnp.logical_and(inside, front_row < front_col))
    def _():
        for js in range(4):
            rs = slice(js * SL, (js + 1) * SL)
            for t in range(4):
                for src in range(4):
                    for half in range(2):
                        lo = src * 2 * H + half * H
                        tile_s[js, t, lo : lo + H, :] = recv_ref[half * 4 + js, t * 4 + src, 0, 0]
                ts = slice(t * SL, (t + 1) * SL)
                out_ref[rs, ts] = tile_s[js, t].T - p_s[rs, ts]

    @pl.when(front_col < 2)
    def _():
        out_ref[...] = panel_ref[...]

    @pl.when(jnp.logical_and(front_row < 2, front_col >= 2))
    def _():
        out_ref[...] = jnp.zeros_like(out_ref)

    @pl.when(jnp.logical_and(inside, front_row == front_col))
    def _():
        for t in range(B // SL):
            ts = slice(t * SL, (t + 1) * SL)
            eye = lax.broadcasted_iota(jnp.int32, (SL, SL), 0) == lax.broadcasted_iota(
                jnp.int32, (SL, SL), 1
            )
            d = diag_ref[front_row, :, ts]
            out_ref[ts, ts] = out_ref[ts, ts] + jnp.where(eye, d, 0.0)


def finish(received, high, low, y, panel, diag):
    rows = pl.BlockSpec((B, W), lambda q, s: (s, 0))
    return pl.pallas_call(
        finish_kernel,
        grid=(2, 4),
        in_specs=[
            pl.BlockSpec((N_ROW, N_COL, 1, 1, H, SL), lambda q, s: (0, 0, s, q, 0, 0)),
            rows,
            rows,
        ]
        + [
            pl.BlockSpec((count, N_COL, 1, 2, H, SL), lambda q, s: (0, 0, q, 0, 0, 0))
            for count in (2, 2, 2, 1, 1)
        ]
        + [
            pl.BlockSpec((B, B), lambda q, s: (s * (1 - q), 0)),
            whole(),
        ],
        out_specs=pl.BlockSpec((B, B), lambda q, s: (s, q)),
        out_shape=jax.ShapeDtypeStruct((4 * B, 2 * B), F32),
        scratch_shapes=[
            VMEM((B, B), F32),
            VMEM((4, 4, SL, SL), F32),
            VMEM((B, W), BF16),
            VMEM((B, W), BF16),
        ],
        compiler_params=params(58),
        cost_estimate=cost(1.3e10, 30 * MIB),
        name="finish",
    )(received, high, low, *y, panel, diag)


def swap(x):
    half_rows = N_ROW // 2
    return lax.ppermute(x, "row", [(i, (i + half_rows) % N_ROW) for i in range(N_ROW)])


def exchange(x, axes):
    return lax.all_to_all(x, axes, split_axis=0, concat_axis=0, tiled=True)


def from_shift(x, axis, stride, shift, side=SIDE):
    pairs = []
    for i in range(N_COL if axis == "col" else N_ROW):
        place = (i // stride) % side
        target = (place - shift) % side
        pairs.append((i, i + (target - place) * stride))
    return lax.ppermute(x, axis, pairs)


def shards(child_fronts, parent_diagonal, block_maps):
    child = child_fronts.transpose(0, 2, 1, 3)
    p_keep, p_send = split_panel(child)
    p_other = swap(p_send)
    r_keep, r_send = split_rest(child)
    r_other = swap(r_send)
    xd, y = panel_pieces(block_maps, p_keep, p_other)

    xd = exchange(xd, "row")
    x = lax.all_gather(xd[:, :8].reshape(N_ROW, 4, 2, H, SL), "col", axis=0, tiled=False)
    d = xd[:, 8:]
    d = jnp.stack([d] + [from_shift(d, "col", 1, shift) for shift in SHIFTS[1:]])
    before, after = from_shift(d, "col", SIDE, 3), from_shift(d, "col", SIDE, 1)
    d = (d, before, after)
    d += (from_shift(before[:2], "col", SIDE, 3), from_shift(after[2:], "col", SIDE, 1))
    y = exchange(y, "col")
    y = jnp.stack([y, from_shift(y, "row", 1, 1, 2)])
    before, after = from_shift(y, "row", 2, 3), from_shift(y, "row", 2, 1)
    y = (y, before, after)
    y += (from_shift(before[:1], "row", 2, 3), from_shift(after[1:], "row", 2, 1))
    packed = pack(block_maps, p_keep, p_other, r_keep, r_other)
    packed, d, y = lax.optimization_barrier((packed, d, y))
    lower, inverse, high, low = cholesky(d, parent_diagonal[: 2 * B].reshape(1, 2 * B))
    high, low, panel = solve_rows(x, inverse, lower, high, low)

    received = exchange(packed.reshape(N_ROW * N_COL, 4, 2, H, SL), ("row", "col"))
    received = received.reshape(N_ROW, N_COL, 4, 2, H, SL)

    return finish(received, high, low, y, panel, parent_diagonal.reshape(NB, 1, B))


def solution(mesh):
    return jax.shard_map(
        shards,
        mesh=mesh,
        in_specs=(P(None, "col", None, "row"), P(), P()),
        out_specs=P("row", "col"),
        check_vma=False,
    )
```
